32 devices in a mesh: ty: 8 (over z, y), tx: 4 (over x, core).
Axes of the slice: x: 2, y: 2, z: 4, core: 2. Of those that a mesh axis runs over, the one named last changes fastest.
Arguments:
- object_field: float32 [3, 2, 1024, 512], P(None, None, 'ty', 'tx'), may hold values from -6 to 6
- probe: float32 [2, 256, 256], replicated, may hold values from -6 to 6
- propagator_phase: float32 [256, 256], replicated, may hold values from -3.140625 to 3.140625
- patterns: float32 [8, 4, 1, 256, 256], P('ty', 'tx'), may hold values from 0 to 2
- scan_positions: int32 [8, 4, 1, 2], P('ty', 'tx'), may hold values from 0 to 255
Outputs:
- updated_object: float32 [3, 2, 1024, 512], P(None, None, 'ty', 'tx')
The draws below stay inside these ranges and needn't reach their ends.
All inputs are finite; a program needn't handle non-finite values.
Results may differ from the reference program's by a relative error of at most 0.0003.
Values sent between devices are 32-bit elements; how exact they have to be, the bound alone decides.
A program may use at most 64 MiB of HBM per device.

```python
import jax
import jax.numpy as jnp
from jax import lax

TILE = 256
MARGIN = 64
SLICES = 3
STEPS = 2
PAT = 1
TILES_Y = 8
TILES_X = 4
NY = 1024
NX = 512


def touch_ends(drawn, own_key, least, largest):
    longest = drawn.shape.index(max(drawn.shape))
    spots = []
    for shift in (0, 1):
        where = [jax.random.randint(jax.random.fold_in(own_key, axis), (), 0, length) for axis, length in enumerate(drawn.shape)]
        where[longest] = (where[longest] + shift) % drawn.shape[longest]
        spots.append(tuple(where))
    return drawn.at[spots[0]].set(least).at[spots[1]].set(largest)


def shard_levels(stream_key, shape, pieces, low, high):
    def one(position, blocks):
        heights = jax.random.uniform(jax.random.fold_in(jax.random.fold_in(stream_key, 6), position), (blocks,), jnp.float32, low / len(pieces), high / len(pieces))
        return jnp.repeat(jnp.exp(heights), shape[position] // blocks).reshape((-1,) + (1,) * (len(shape) - position - 1))

    factor_of = one(*pieces[0])
    for cut in pieces[1:]:
        factor_of = factor_of * one(*cut)
    return factor_of


def gaussian(key, shape, spread, bound, cuts=(), kind=jnp.bfloat16):
    factor_of = shard_levels(key, shape, cuts, -0.22, 0.18) if cuts else 1.0
    array = jax.random.normal(key, shape, jnp.float32) * spread * factor_of
    return jnp.minimum(jnp.maximum(array, -bound), bound).astype(kind)


def setup_inputs(seed: int = 0) -> dict:
    arg_keys = jax.random.split(jax.random.key(seed), 6)
    object_field = gaussian(arg_keys[0], (SLICES, 2, NY, NX), 0.7, 6.0, ((2, 8), (3, 4)), jnp.float32)
    probe = gaussian(arg_keys[1], (2, TILE, TILE), 0.7, 6.0, (), jnp.float32)
    propagator_phase = jnp.clip(jax.random.uniform(arg_keys[2], (TILE, TILE), jnp.float32, -3.140625, 3.140625), -3.140625, 3.140625)
    patterns = jnp.clip(2.0 * jax.random.uniform(arg_keys[3], (TILES_Y, TILES_X, PAT, TILE, TILE), jnp.float32) ** shard_levels(arg_keys[3], (TILES_Y, TILES_X, PAT, TILE, TILE), ((0, 8), (1, 4)), -0.2, 0.2), 0.0, 2.0)
    scan_positions = touch_ends(jax.random.randint(arg_keys[4], (TILES_Y, TILES_X, PAT, 2), 0, TILE), jax.random.fold_in(arg_keys[4], 1), 0, TILE - 1).astype(jnp.int32)
    return {"object_field": object_field, "probe": probe, "propagator_phase": propagator_phase, "patterns": patterns, "scan_positions": scan_positions}


step_size = 0.05


def forward_dft(field):
    return jnp.fft.fft2(field, axes=(-2, -1), norm="ortho")


def inverse_dft(field):
    return jnp.fft.ifft2(field, axes=(-2, -1), norm="ortho")


def tile_gradient(tile, tile_patterns, positions, probe, kernel):
    slices = [lax.complex(tile[layer, 0], tile[layer, 1]) for layer in range(SLICES)]
    gradients = [jnp.zeros_like(slices[0]) for layer in range(SLICES)]
    for pattern_index in range(PAT):
        shift_rows = positions[pattern_index, 0]
        shift_cols = positions[pattern_index, 1]
        probe_real = jnp.roll(probe[0], (shift_rows, shift_cols), axis=(0, 1))
        probe_imag = jnp.roll(probe[1], (shift_rows, shift_cols), axis=(0, 1))
        lit = lax.complex(probe_real, probe_imag)
        wave = lit * slices[0]
        entering = []
        for layer in range(1, SLICES):
            moved = inverse_dft(kernel * forward_dft(wave))
            entering.append(moved)
            wave = moved * slices[layer]
        far_field = forward_dft(wave)
        power = jnp.real(far_field) ** 2 + jnp.imag(far_field) ** 2
        upstream = inverse_dft((power - tile_patterns[pattern_index]) * far_field)
        for layer in range(SLICES - 1, 0, -1):
            gradients[layer] = gradients[layer] + jnp.conj(entering[layer - 1]) * upstream
            upstream = inverse_dft(jnp.conj(kernel) * forward_dft(jnp.conj(slices[layer]) * upstream))
        gradients[0] = gradients[0] + jnp.conj(lit) * upstream
    return jnp.stack([jnp.stack([jnp.real(grad), jnp.imag(grad)]) for grad in gradients])


def shift_tiles(grid, offset, axis):
    zeros = jnp.zeros_like(lax.slice_in_dim(grid, 0, 1, axis=axis))
    if offset == 1:
        return jnp.concatenate([zeros, lax.slice_in_dim(grid, 0, grid.shape[axis] - 1, axis=axis)], axis=axis)
    return jnp.concatenate([lax.slice_in_dim(grid, 1, grid.shape[axis], axis=axis), zeros], axis=axis)


def owner_sum(grid, tile_axis, pixel_axis):
    core = TILE - 2 * MARGIN
    middle = lax.slice_in_dim(grid, MARGIN, MARGIN + core, axis=pixel_axis)
    from_above = lax.slice_in_dim(shift_tiles(grid, 1, tile_axis), TILE - MARGIN, TILE, axis=pixel_axis)
    from_below = lax.slice_in_dim(shift_tiles(grid, -1, tile_axis), 0, MARGIN, axis=pixel_axis)
    widths_above = [(0, 0)] * grid.ndim
    widths_above[pixel_axis] = (0, core - MARGIN)
    widths_below = [(0, 0)] * grid.ndim
    widths_below[pixel_axis] = (core - MARGIN, 0)
    return middle + jnp.pad(from_above, widths_above) + jnp.pad(from_below, widths_below)


def reference(object_field, probe, propagator_phase, patterns, scan_positions):
    kernel = lax.complex(jnp.cos(propagator_phase), jnp.sin(propagator_phase))
    core = TILE - 2 * MARGIN
    current = object_field
    for iteration in range(STEPS):
        padded = jnp.pad(current, ((0, 0), (0, 0), (MARGIN, MARGIN), (MARGIN, MARGIN)))

        def one_tile(flat_index):
            tile_row = flat_index // TILES_X
            tile_col = flat_index % TILES_X
            zero = jnp.zeros((), jnp.int32)
            tile = lax.dynamic_slice(padded, (zero, zero, (tile_row * core).astype(jnp.int32), (tile_col * core).astype(jnp.int32)), (SLICES, 2, TILE, TILE))
            return tile_gradient(tile, patterns[tile_row, tile_col], scan_positions[tile_row, tile_col], probe, kernel)

        grads = lax.map(one_tile, jnp.arange(TILES_Y * TILES_X, dtype=jnp.int32))
        grads = grads.reshape(TILES_Y, TILES_X, SLICES, 2, TILE, TILE)
        summed = owner_sum(grads, 0, 4)
        summed = owner_sum(summed, 1, 5)
        summed = jnp.transpose(summed, (2, 3, 0, 4, 1, 5)).reshape(SLICES, 2, TILES_Y * core, TILES_X * core)
        current = current - step_size * summed
    return current
```

```python
import functools

import jax
import jax.numpy as jnp
import ml_dtypes
import numpy as np
from jax import lax
from jax.experimental import pallas as pl
from jax.experimental.pallas import tpu as pltpu
from jax.sharding import PartitionSpec as P

STEPS = 2

step_size = 0.05


def dft_tables(n):
    h = n // 2
    place = np.arange(h)
    tables = []
    for parity in (0, 1):
        turns = ((2 * place[:, None] + parity) * place[None, :]) % n
        angle = turns * (2.0 * np.pi / n)
        c = np.cos(angle) / np.sqrt(n)
        s = -np.sin(angle) / np.sqrt(n)
        block = np.block([[c, -s], [s, c]])
        for full in (block, block.T):
            high = full.astype(ml_dtypes.bfloat16)
            low = (full - high.astype(np.float64)).astype(ml_dtypes.bfloat16)
            tables += [high, low]
    return np.stack(tables)


def split2(x):
    high = x.astype(jnp.bfloat16)
    low = (x - high.astype(jnp.float32)).astype(jnp.bfloat16)
    return high, low


def split3(x):
    high = x.astype(jnp.bfloat16)
    rest = x - high.astype(jnp.float32)
    middle = rest.astype(jnp.bfloat16)
    low = (rest - middle.astype(jnp.float32)).astype(jnp.bfloat16)
    return high, middle, low


def dot(a, b):
    return jnp.dot(a, b, preferred_element_type=jnp.float32)


def cat(parts, axis):
    return jnp.concatenate(parts, axis=axis)


def cmul(a, b):
    return (a[0] * b[0] - a[1] * b[1], a[0] * b[1] + a[1] * b[0])


def cmul_conj(a, b):
    return (a[0] * b[0] + a[1] * b[1], a[0] * b[1] - a[1] * b[0])


def sin_cos(x):
    y = x * 0.5
    z = y * y
    s = jnp.float32(-2.50521083854417e-08)
    for c in (2.75573192239859e-06, -1.98412698412698e-04, 8.33333333333333e-03, -1.66666666666667e-01):
        s = s * z + jnp.float32(c)
    s = s * z * y + y
    c0 = jnp.float32(2.08767569878681e-09)
    for c in (-2.75573192239859e-07, 2.48015873015873e-05, -1.38888888888889e-03, 4.16666666666667e-02, -0.5):
        c0 = c0 * z + jnp.float32(c)
    c0 = c0 * z + 1.0
    return 2.0 * s * c0, 1.0 - 2.0 * s * s


def kernel(
    pos_ref, obj_ref, probe_ref, phase_ref, pat_ref, tab_ref, out_ref,
    tile, lit, hk, pat, wave, grad, rim, sendx, recvx, recvy, recvl,
    sem_s, sem_r,
):
    slices = obj_ref.shape[0]
    core = obj_ref.shape[2]
    n = probe_ref.shape[1]
    h = n // 2
    m = (n - core) // 2
    ty, tx = lax.axis_index("ty"), lax.axis_index("tx")
    ny, nx = lax.axis_size("ty"), lax.axis_size("tx")
    near = {
        "ty": ((ty > 0, (ty - 1, tx)), (ty < ny - 1, (ty + 1, tx))),
        "tx": ((tx > 0, (ty, tx - 1)), (tx < nx - 1, (ty, tx + 1))),
    }
    pending = []

    def copy_of(axis, side, src, dst, slot):
        return pltpu.make_async_remote_copy(
            src_ref=src, dst_ref=dst,
            send_sem=sem_s.at[slot], recv_sem=sem_r.at[slot],
            device_id=near[axis][side][1], device_id_type=pl.DeviceIdType.MESH,
        )

    def send(axis, side, src, dst, slot):
        @pl.when(near[axis][side][0])
        def _():
            copy_of(axis, side, src, dst, slot).start()

        pending.append((axis, side, src, dst, slot))

    def arrive(axis, side, src, dst, slot):
        @pl.when(near[axis][1 - side][0])
        def _():
            copy_of(axis, 1 - side, src, dst, slot).wait_recv()

    def slot_of(phase, layer, side):
        return (phase * slices + layer) * 2 + side

    barrier = pltpu.get_barrier_semaphore()
    count = jnp.int32(0)
    for axis in ("ty", "tx"):
        for there, device in near[axis]:
            @pl.when(there)
            def _():
                pl.semaphore_signal(barrier, inc=1, device_id=device, device_id_type=pl.DeviceIdType.MESH)
            count = count + there.astype(jnp.int32)
    pl.semaphore_wait(barrier, count)

    after, before = pl.ds(core, m), pl.ds(core + m, m)
    head, tail = pl.ds(0, m), pl.ds(core - m, m)
    own = pl.ds(0, core)
    other = pl.ds(core, core)

    def rim_rows(layer):
        return (
            (obj_ref.at[layer, :, head, :], tile.at[layer, :, after, own]),
            (obj_ref.at[layer, :, tail, :], tile.at[layer, :, before, own]),
        )

    for layer in range(slices):
        for side in (0, 1):
            src, dst = rim_rows(layer)[side]
            send("ty", side, src, dst, slot_of(0, layer, side))

    tile[:, :, own, own] = obj_ref[...]

    @pl.when(ty == 0)
    def _():
        tile[:, :, before, own] = jnp.zeros((slices, 2, m, core), jnp.float32)
        recvy[:, 1] = jnp.zeros(recvy.shape[:1] + recvy.shape[2:], jnp.float32)
        recvl[:, 1] = jnp.zeros(recvl.shape[:1] + recvl.shape[2:], jnp.float32)

    @pl.when(ty == ny - 1)
    def _():
        tile[:, :, after, own] = jnp.zeros((slices, 2, m, core), jnp.float32)
        recvy[:, 0] = jnp.zeros(recvy.shape[:1] + recvy.shape[2:], jnp.float32)
        recvl[:, 0] = jnp.zeros(recvl.shape[:1] + recvl.shape[2:], jnp.float32)

    @pl.when(tx == 0)
    def _():
        for phase in range(recvx.shape[0]):
            recvx[phase, :, 1] = jnp.zeros(recvx.shape[1:2] + recvx.shape[3:], jnp.float32)

    @pl.when(tx == nx - 1)
    def _():
        for phase in range(recvx.shape[0]):
            recvx[phase, :, 0] = jnp.zeros(recvx.shape[1:2] + recvx.shape[3:], jnp.float32)

    first_half = lax.broadcasted_iota(jnp.int32, (h, core), 1) < m

    def turn(x):
        return pltpu.roll(x, m, 1)

    def pack(block):
        top, bottom = block[:h], block[h:]
        return (
            jnp.where(first_half, top, turn(bottom)),
            jnp.where(first_half, turn(top), bottom),
        )

    def unpack(low, high):
        return (
            jnp.where(first_half, low, turn(high)),
            jnp.where(first_half, turn(low), high),
        )

    def send_strips(phase, layer, part, low, high, low_side):
        sendx[phase, layer, low_side, part] = low
        sendx[phase, layer, 1 - low_side, part] = high

    def start_strips(phase, layer):
        for side in (0, 1):
            send("tx", side, sendx.at[phase, layer, side], recvx.at[phase, layer, side], slot_of(2 * phase + 1, layer, side))

    def wait_strips(phase, layer):
        for side in (0, 1):
            arrive("tx", side, sendx.at[phase, layer, side], recvx.at[phase, layer, side], slot_of(2 * phase + 1, layer, side))

    def send_columns(phase, layer):
        for part in (0, 1):
            low, high = pack(tile[layer, part, :, own])
            send_strips(phase, layer, part, low, high, 0)
        start_strips(phase, layer)

    def place_columns(phase, layer):
        wait_strips(phase, layer)
        for part in (0, 1):
            top, bottom = unpack(recvx[phase, layer, 0, part], recvx[phase, layer, 1, part])
            tile[layer, part, pl.ds(0, h), other] = top
            tile[layer, part, pl.ds(h, h), other] = bottom

    def send_gradient(phase, layer, g):
        for part in (0, 1):
            grad[layer, part, pl.ds(0, n)] = g[part][:, :core]
            low, high = pack(g[part][:, core:])
            send_strips(phase, layer, part, low, high, 1)
        start_strips(phase, layer)

    def sum_columns(phase, layer):
        wait_strips(phase, layer)
        for part in (0, 1):
            top, bottom = unpack(recvx[phase, layer, 1, part], recvx[phase, layer, 0, part])
            top = grad[layer, part, pl.ds(0, h)] + top
            rim[phase, layer, part, pl.ds(0, h)] = top
            rim[phase, layer, part, pl.ds(h, h)] = grad[layer, part, pl.ds(h, h)] + bottom
            rim[phase, layer, part, pl.ds(n, m)] = top[:m]

    def middle_rows(layer):
        return (
            (rim.at[1, layer, :, pl.ds(core + m, 2 * m), :], recvy.at[layer, 0]),
            (rim.at[1, layer, :, pl.ds(core - m, 2 * m), :], recvy.at[layer, 1]),
        )

    def last_rows(layer):
        return (
            (rim.at[3, layer, :, pl.ds(core + m, m), :], recvl.at[layer, 0]),
            (rim.at[3, layer, :, pl.ds(core, m), :], recvl.at[layer, 1]),
        )

    def send_rows(rows, phase, layer):
        for side in (0, 1):
            src, dst = rows(layer)[side]
            send("ty", side, src, dst, slot_of(phase, layer, side))

    def wait_rows(rows, phase, layer):
        for side in (0, 1):
            src, dst = rows(layer)[side]
            arrive("ty", side, src, dst, slot_of(phase, layer, side))

    def update_middle(layer):
        wait_rows(middle_rows, 2, layer)
        for part in (0, 1):
            for start, side, at in ((0, 1, m), (m, 0, 0), (2 * m, 0, m), (3 * m, 1, 0)):
                rows = pl.ds(start, m)
                total = rim[1, layer, part, rows] + recvy[layer, side, part, pl.ds(at, m)]
                tile[layer, part, rows, own] = tile[layer, part, rows, own] - step_size * total

        @pl.when(ty == 0)
        def _():
            tile[layer, :, before, own] = jnp.zeros((2, m, core), jnp.float32)

        @pl.when(ty == ny - 1)
        def _():
            tile[layer, :, after, own] = jnp.zeros((2, m, core), jnp.float32)

    def update_last(layer):
        wait_rows(last_rows, 4, layer)
        for part in (0, 1):
            for start, side in ((0, 1), (m, 0)):
                rows = pl.ds(start, m)
                total = rim[3, layer, part, rows] + recvl[layer, side, part]
                out_ref[layer, part, rows] = tile[layer, part, rows, own] - step_size * total

    row = lax.broadcasted_iota(jnp.int32, (n, n), 0)
    col = lax.broadcasted_iota(jnp.int32, (n, n), 1)

    def ones(mask):
        return jnp.where(mask, 1.0, 0.0).astype(jnp.bfloat16)

    def pick(left, x, right):
        a, b, c = split3(x)
        y = dot(left, a) + dot(left, b) + dot(left, c)
        a, b, c = split3(y)
        return dot(a, right) + dot(b, right) + dot(c, right)

    def rolled(i, j, shift):
        d = i - j + (m - shift + n)
        return ones((d == 0) | (d == n) | (d == 2 * n))

    roll_rows = rolled(row, col, pos_ref[0, 0, 0, 0])
    roll_cols = rolled(col, row, pos_ref[0, 0, 0, 1])
    for part in (0, 1):
        lit[part] = pick(roll_rows, probe_ref[part], roll_cols)

    def sorted_by_parity(i, j):
        return ones(jnp.where(i < h, 2 * i, 2 * i - n + 1) == j)

    by_row, by_col = sorted_by_parity(row, col), sorted_by_parity(col, row)
    pat[...] = pick(by_row, pat_ref[...], by_col)
    sine, cosine = sin_cos(pick(by_row, phase_ref[...], by_col))
    hk[0] = cosine
    hk[1] = sine

    EVEN, EVEN_T, ODD, ODD_T = 0, 2, 4, 6

    def from_left(table, x):
        high, low = tab_ref[table], tab_ref[table + 1]
        xh, xl = split2(x)
        return dot(cat([high, high, low], 1), cat([xh, xl, xh], 0))

    def from_right(x, table):
        high, low = tab_ref[table], tab_ref[table + 1]
        xh, xl = split2(x)
        return dot(cat([xh, xl, xh], 1), cat([high, high, low], 0))

    def through(field, weigh):
        re, im = field
        even = from_left(EVEN, cat([re[:h] + re[h:], im[:h] + im[h:]], 0))
        odd = from_left(ODD, cat([re[:h] - re[h:], im[:h] - im[h:]], 0))
        re = cat([even[:h], odd[:h]], 0)
        im = cat([even[h:], odd[h:]], 0)
        even = from_right(cat([re[:, :h] + re[:, h:], im[:, :h] + im[:, h:]], 1), EVEN_T)
        odd = from_right(cat([re[:, :h] - re[:, h:], im[:, :h] - im[:, h:]], 1), ODD_T)
        even = cat(weigh((even[:, :h], even[:, h:]), pl.ds(0, h)), 1)
        odd = cat(weigh((odd[:, :h], odd[:, h:]), pl.ds(h, h)), 1)
        even = from_right(even, EVEN)
        odd = from_right(odd, ODD)
        first, second = even + odd, even - odd
        re = cat([first[:, :h], second[:, :h]], 1)
        im = cat([first[:, h:], second[:, h:]], 1)
        even = from_left(EVEN_T, cat([re[:h], im[:h]], 0))
        odd = from_left(ODD_T, cat([re[h:], im[h:]], 0))
        first, second = even + odd, even - odd
        return cat([first[:h], second[:h]], 0), cat([first[h:], second[h:]], 0)

    def forward_kernel(f, cols):
        return cmul((hk[0, :, cols], hk[1, :, cols]), f)

    def backward_kernel(f, cols):
        return cmul_conj((hk[0, :, cols], hk[1, :, cols]), f)

    def residue(f, cols):
        g = f[0] * f[0] + f[1] * f[1] - pat[:, cols]
        return g * f[0], g * f[1]

    def pair(ref, *at):
        return (ref[(*at, 0)], ref[(*at, 1)])

    def entering(layer):
        return pair(lit) if layer == 0 else pair(wave, layer - 1)

    for layer in range(slices):
        for side in (0, 1):
            src, dst = rim_rows(layer)[side]
            arrive("ty", side, src, dst, slot_of(0, layer, side))
        send_columns(0, layer)

    for step in range(STEPS):
        columns, strips = 2 * step, 2 * step + 1
        last = step == STEPS - 1
        rows, phase = (last_rows, 4) if last else (middle_rows, 2)
        for layer in range(slices - 1):
            place_columns(columns, layer)
            moved = through(cmul(entering(layer), pair(tile, layer)), forward_kernel)
            wave[layer, 0] = moved[0]
            wave[layer, 1] = moved[1]
        layer = slices - 1
        place_columns(columns, layer)
        up = through(cmul(entering(layer), pair(tile, layer)), residue)
        for layer in range(slices - 1, -1, -1):
            send_gradient(strips, layer, cmul_conj(entering(layer), up))
            if layer < slices - 1:
                sum_columns(strips, layer + 1)
                send_rows(rows, phase, layer + 1)
            if layer > 0:
                up = through(cmul_conj(pair(tile, layer), up), backward_kernel)
        sum_columns(strips, 0)
        send_rows(rows, phase, 0)
        for layer in range(slices - 1, -1, -1):
            if last:
                update_last(layer)
            else:
                update_middle(layer)
                send_columns(columns + 2, layer)

    for axis, side, src, dst, slot in pending:
        @pl.when(near[axis][side][0])
        def _():
            copy_of(axis, side, src, dst, slot).wait_send()


def shards(object_field, probe, propagator_phase, patterns, scan_positions):
    slices, _, core, _ = object_field.shape
    n = probe.shape[1]
    m = (n - core) // 2
    f32 = jnp.float32
    tables = jnp.asarray(dft_tables(n))
    vmem = pl.BlockSpec(memory_space=pltpu.VMEM)
    slots = 8 * slices * 2
    return pl.pallas_call(
        kernel,
        out_shape=jax.ShapeDtypeStruct(object_field.shape, f32),
        in_specs=[pl.BlockSpec(memory_space=pltpu.SMEM)] + [vmem] * 5,
        out_specs=vmem,
        scratch_shapes=[
            pltpu.VMEM((slices, 2, n, n), f32),
            pltpu.VMEM((2, n, n), f32),
            pltpu.VMEM((2, n, n), f32),
            pltpu.VMEM((n, n), f32),
            pltpu.VMEM((slices - 1, 2, n, n), f32),
            pltpu.VMEM((slices, 2, n, core), f32),
            pltpu.VMEM((2 * STEPS, slices, 2, n + m, core), f32),
            pltpu.VMEM((2 * STEPS, slices, 2, 2, n // 2, core), f32),
            pltpu.VMEM((2 * STEPS, slices, 2, 2, n // 2, core), f32),
            pltpu.VMEM((slices, 2, 2, 2 * m, core), f32),
            pltpu.VMEM((slices, 2, 2, m, core), f32),
            pltpu.SemaphoreType.DMA((slots,)),
            pltpu.SemaphoreType.DMA((slots,)),
        ],
        compiler_params=pltpu.CompilerParams(
            collective_id=0, has_side_effects=True, vmem_limit_bytes=48 * 1024 * 1024
        ),
        name="steps",
    )(scan_positions, object_field, probe, propagator_phase, patterns[0, 0, 0], tables)


def solution(mesh):
    placed = (
        P(None, None, "ty", "tx"),
        P(),
        P(),
        P("ty", "tx", None, None, None),
        P("ty", "tx", None, None),
    )
    return jax.shard_map(
        shards, mesh=mesh, in_specs=placed, out_specs=P(None, None, "ty", "tx"), check_vma=False
    )
```

```python
import functools

import jax
import jax.numpy as jnp
import ml_dtypes
import numpy as np
from jax import lax
from jax.experimental import pallas as pl
from jax.experimental.pallas import tpu as pltpu
from jax.sharding import PartitionSpec as P

STEPS = 2

step_size = 0.05


def dft_tables(n):
    h = n // 2
    place = np.arange(h)
    tables = []
    for parity in (0, 1):
        turns = ((2 * place[:, None] + parity) * place[None, :]) % n
        angle = turns * (2.0 * np.pi / n)
        c = np.cos(angle) / np.sqrt(n)
        s = -np.sin(angle) / np.sqrt(n)
        block = np.block([[c, -s], [s, c]])
        for full in (block, block.T):
            high = full.astype(ml_dtypes.bfloat16)
            low = (full - high.astype(np.float64)).astype(ml_dtypes.bfloat16)
            tables += [high, low]
    return np.stack(tables)


def split2(x):
    high = x.astype(jnp.bfloat16)
    low = (x - high.astype(jnp.float32)).astype(jnp.bfloat16)
    return high, low


def split3(x):
    high = x.astype(jnp.bfloat16)
    rest = x - high.astype(jnp.float32)
    middle = rest.astype(jnp.bfloat16)
    low = (rest - middle.astype(jnp.float32)).astype(jnp.bfloat16)
    return high, middle, low


def dot(a, b):
    return jnp.dot(a, b, preferred_element_type=jnp.float32)


def cat(parts, axis):
    return jnp.concatenate(parts, axis=axis)


def cmul(a, b):
    return (a[0] * b[0] - a[1] * b[1], a[0] * b[1] + a[1] * b[0])


def cmul_conj(a, b):
    return (a[0] * b[0] + a[1] * b[1], a[0] * b[1] - a[1] * b[0])


def sin_cos(x):
    y = x * 0.5
    z = y * y
    s = jnp.float32(-2.50521083854417e-08)
    for c in (2.75573192239859e-06, -1.98412698412698e-04, 8.33333333333333e-03, -1.66666666666667e-01):
        s = s * z + jnp.float32(c)
    s = s * z * y + y
    c0 = jnp.float32(2.08767569878681e-09)
    for c in (-2.75573192239859e-07, 2.48015873015873e-05, -1.38888888888889e-03, 4.16666666666667e-02, -0.5):
        c0 = c0 * z + jnp.float32(c)
    c0 = c0 * z + 1.0
    return 2.0 * s * c0, 1.0 - 2.0 * s * s


def kernel(
    pos_ref, obj_ref, probe_hbm, phase_hbm, pat_hbm, tab_hbm, out_ref,
    tile, lit, hk, pat, wave, grad, rim, sendx, recvx, recvy, recvl,
    probe_ref, tab_ref, sem_s, sem_r, sem_in,
):
    slices = obj_ref.shape[0]
    core = obj_ref.shape[2]
    n = probe_ref.shape[1]
    h = n // 2
    m = (n - core) // 2
    ty, tx = lax.axis_index("ty"), lax.axis_index("tx")
    ny, nx = lax.axis_size("ty"), lax.axis_size("tx")
    near = {
        "ty": ((ty > 0, (ty - 1, tx)), (ty < ny - 1, (ty + 1, tx))),
        "tx": ((tx > 0, (ty, tx - 1)), (tx < nx - 1, (ty, tx + 1))),
    }
    pending = []

    def copy_of(axis, side, src, dst, slot):
        return pltpu.make_async_remote_copy(
            src_ref=src, dst_ref=dst,
            send_sem=sem_s.at[slot], recv_sem=sem_r.at[slot],
            device_id=near[axis][side][1], device_id_type=pl.DeviceIdType.MESH,
        )

    def send(axis, side, src, dst, slot):
        @pl.when(near[axis][side][0])
        def _():
            copy_of(axis, side, src, dst, slot).start()

        pending.append((axis, side, src, dst, slot))

    def arrive(axis, side, src, dst, slot):
        @pl.when(near[axis][1 - side][0])
        def _():
            copy_of(axis, 1 - side, src, dst, slot).wait_recv()

    def slot_of(phase, layer, side):
        return (phase * slices + layer) * 2 + side

    fetch_core, fetch_probe, fetch_phase, fetch_pat, fetch_tab = (
        pltpu.make_async_copy(src, dst, sem_in.at[i])
        for i, (src, dst) in enumerate((
            (obj_ref, tile.at[:, :, pl.ds(0, core), pl.ds(0, core)]),
            (probe_hbm, probe_ref),
            (phase_hbm, hk.at[0]),
            (pat_hbm.at[0, 0, 0], pat),
            (tab_hbm, tab_ref),
        ))
    )
    for fetch in (fetch_core, fetch_probe, fetch_phase, fetch_pat, fetch_tab):
        fetch.start()

    barrier = pltpu.get_barrier_semaphore()
    count = jnp.int32(0)
    for axis in ("ty", "tx"):
        for there, device in near[axis]:
            @pl.when(there)
            def _():
                pl.semaphore_signal(barrier, inc=1, device_id=device, device_id_type=pl.DeviceIdType.MESH)
            count = count + there.astype(jnp.int32)
    pl.semaphore_wait(barrier, count)

    after, before = pl.ds(core, m), pl.ds(core + m, m)
    head, tail = pl.ds(0, m), pl.ds(core - m, m)
    own = pl.ds(0, core)
    other = pl.ds(core, core)

    def rim_rows(layer):
        return (
            (obj_ref.at[layer, :, head, :], tile.at[layer, :, after, own]),
            (obj_ref.at[layer, :, tail, :], tile.at[layer, :, before, own]),
        )

    for layer in range(slices):
        for side in (0, 1):
            src, dst = rim_rows(layer)[side]
            send("ty", side, src, dst, slot_of(0, layer, side))

    @pl.when(ty == 0)
    def _():
        tile[:, :, before, own] = jnp.zeros((slices, 2, m, core), jnp.float32)
        recvy[:, 1] = jnp.zeros(recvy.shape[:1] + recvy.shape[2:], jnp.float32)
        recvl[:, 1] = jnp.zeros(recvl.shape[:1] + recvl.shape[2:], jnp.float32)

    @pl.when(ty == ny - 1)
    def _():
        tile[:, :, after, own] = jnp.zeros((slices, 2, m, core), jnp.float32)
        recvy[:, 0] = jnp.zeros(recvy.shape[:1] + recvy.shape[2:], jnp.float32)
        recvl[:, 0] = jnp.zeros(recvl.shape[:1] + recvl.shape[2:], jnp.float32)

    @pl.when(tx == 0)
    def _():
        for phase in range(recvx.shape[0]):
            recvx[phase, :, 1] = jnp.zeros(recvx.shape[1:2] + recvx.shape[3:], jnp.float32)

    @pl.when(tx == nx - 1)
    def _():
        for phase in range(recvx.shape[0]):
            recvx[phase, :, 0] = jnp.zeros(recvx.shape[1:2] + recvx.shape[3:], jnp.float32)

    first_half = lax.broadcasted_iota(jnp.int32, (h, core), 1) < m

    def turn(x):
        return pltpu.roll(x, m, 1)

    def pack(block):
        top, bottom = block[:h], block[h:]
        return (
            jnp.where(first_half, top, turn(bottom)),
            jnp.where(first_half, turn(top), bottom),
        )

    def unpack(low, high):
        return (
            jnp.where(first_half, low, turn(high)),
            jnp.where(first_half, turn(low), high),
        )

    def send_strips(phase, layer, part, low, high, low_side):
        sendx[phase, layer, low_side, part] = low
        sendx[phase, layer, 1 - low_side, part] = high

    def start_strips(phase, layer):
        for side in (0, 1):
            send("tx", side, sendx.at[phase, layer, side], recvx.at[phase, layer, side], slot_of(2 * phase + 1, layer, side))

    def wait_strips(phase, layer):
        for side in (0, 1):
            arrive("tx", side, sendx.at[phase, layer, side], recvx.at[phase, layer, side], slot_of(2 * phase + 1, layer, side))

    def send_columns(phase, layer):
        for part in (0, 1):
            low, high = pack(tile[layer, part, :, own])
            send_strips(phase, layer, part, low, high, 0)
        start_strips(phase, layer)

    def place_columns(phase, layer):
        wait_strips(phase, layer)
        for part in (0, 1):
            top, bottom = unpack(recvx[phase, layer, 0, part], recvx[phase, layer, 1, part])
            tile[layer, part, pl.ds(0, h), other] = top
            tile[layer, part, pl.ds(h, h), other] = bottom

    def send_gradient(phase, layer, g):
        for part in (0, 1):
            grad[layer, part, pl.ds(0, n)] = g[part][:, :core]
            low, high = pack(g[part][:, core:])
            send_strips(phase, layer, part, low, high, 1)
        start_strips(phase, layer)

    def sum_columns(phase, layer):
        wait_strips(phase, layer)
        for part in (0, 1):
            top, bottom = unpack(recvx[phase, layer, 1, part], recvx[phase, layer, 0, part])
            top = grad[layer, part, pl.ds(0, h)] + top
            rim[phase, layer, part, pl.ds(0, h)] = top
            rim[phase, layer, part, pl.ds(h, h)] = grad[layer, part, pl.ds(h, h)] + bottom
            rim[phase, layer, part, pl.ds(n, m)] = top[:m]

    def middle_rows(layer, part):
        return (
            (rim.at[1, layer, part, pl.ds(core + m, 2 * m), :], recvy.at[layer, 0, part]),
            (rim.at[1, layer, part, pl.ds(core - m, 2 * m), :], recvy.at[layer, 1, part]),
        )

    def last_rows(layer):
        return (
            (rim.at[3, layer, :, pl.ds(core + m, m), :], recvl.at[layer, 0]),
            (rim.at[3, layer, :, pl.ds(core, m), :], recvl.at[layer, 1]),
        )

    def send_middle(layer, part):
        for side in (0, 1):
            src, dst = middle_rows(layer, part)[side]
            send("ty", side, src, dst, slot_of((2, 6)[part], layer, side))

    def send_last(layer):
        for side in (0, 1):
            src, dst = last_rows(layer)[side]
            send("ty", side, src, dst, slot_of(4, layer, side))

    def update_middle(layer):
        for part in (0, 1):
            for side in (0, 1):
                src, dst = middle_rows(layer, part)[side]
                arrive("ty", side, src, dst, slot_of((2, 6)[part], layer, side))
            for start, side, at in ((0, 1, m), (m, 0, 0), (2 * m, 0, m), (3 * m, 1, 0)):
                rows = pl.ds(start, m)
                total = rim[1, layer, part, rows] + recvy[layer, side, part, pl.ds(at, m)]
                tile[layer, part, rows, own] = tile[layer, part, rows, own] - step_size * total

        @pl.when(ty == 0)
        def _():
            tile[layer, :, before, own] = jnp.zeros((2, m, core), jnp.float32)

        @pl.when(ty == ny - 1)
        def _():
            tile[layer, :, after, own] = jnp.zeros((2, m, core), jnp.float32)

    def update_last(layer):
        for side in (0, 1):
            src, dst = last_rows(layer)[side]
            arrive("ty", side, src, dst, slot_of(4, layer, side))
        for part in (0, 1):
            for start, side in ((0, 1), (m, 0)):
                rows = pl.ds(start, m)
                total = rim[3, layer, part, rows] + recvl[layer, side, part]
                out_ref[layer, part, rows] = tile[layer, part, rows, own] - step_size * total

    row = lax.broadcasted_iota(jnp.int32, (n, n), 0)
    col = lax.broadcasted_iota(jnp.int32, (n, n), 1)

    def ones(mask):
        return jnp.where(mask, 1.0, 0.0).astype(jnp.bfloat16)

    def pick(left, x, right):
        a, b, c = split3(x)
        y = dot(left, a) + dot(left, b) + dot(left, c)
        a, b, c = split3(y)
        return dot(a, right) + dot(b, right) + dot(c, right)

    def rolled(i, j, shift):
        d = i - j + (m - shift + n)
        return ones((d == 0) | (d == n) | (d == 2 * n))

    def sorted_by_parity(i, j):
        return ones(jnp.where(i < h, 2 * i, 2 * i - n + 1) == j)

    def prepare_probe():
        fetch_probe.wait()
        roll_rows = rolled(row, col, pos_ref[0, 0, 0, 0])
        roll_cols = rolled(col, row, pos_ref[0, 0, 0, 1])
        for part in (0, 1):
            lit[part] = pick(roll_rows, probe_ref[part], roll_cols)

    def prepare_frequencies():
        by_row, by_col = sorted_by_parity(row, col), sorted_by_parity(col, row)
        fetch_phase.wait()
        sine, cosine = sin_cos(pick(by_row, hk[0], by_col))
        hk[0] = cosine
        hk[1] = sine
        fetch_pat.wait()
        pat[...] = pick(by_row, pat[...], by_col)

    EVEN, EVEN_T, ODD, ODD_T = 0, 2, 4, 6

    def from_left(table, x):
        high, low = tab_ref[table], tab_ref[table + 1]
        xh, xl = split2(x)
        return dot(cat([high, high, low], 1), cat([xh, xl, xh], 0))

    def from_right(x, table):
        high, low = tab_ref[table], tab_ref[table + 1]
        xh, xl = split2(x)
        return dot(cat([xh, xl, xh], 1), cat([high, high, low], 0))

    def through(field, weigh):
        re, im = field
        even = from_left(EVEN, cat([re[:h] + re[h:], im[:h] + im[h:]], 0))
        odd = from_left(ODD, cat([re[:h] - re[h:], im[:h] - im[h:]], 0))
        re = cat([even[:h], odd[:h]], 0)
        im = cat([even[h:], odd[h:]], 0)
        even = from_right(cat([re[:, :h] + re[:, h:], im[:, :h] + im[:, h:]], 1), EVEN_T)
        odd = from_right(cat([re[:, :h] - re[:, h:], im[:, :h] - im[:, h:]], 1), ODD_T)
        even = cat(weigh((even[:, :h], even[:, h:]), pl.ds(0, h)), 1)
        odd = cat(weigh((odd[:, :h], odd[:, h:]), pl.ds(h, h)), 1)
        even = from_right(even, EVEN)
        odd = from_right(odd, ODD)
        first, second = even + odd, even - odd
        re = cat([first[:, :h], second[:, :h]], 1)
        im = cat([first[:, h:], second[:, h:]], 1)
        even = from_left(EVEN_T, cat([re[:h], im[:h]], 0))
        odd = from_left(ODD_T, cat([re[h:], im[h:]], 0))
        first, second = even + odd, even - odd
        return cat([first[:h], second[:h]], 0), cat([first[h:], second[h:]], 0)

    def forward_kernel(f, cols):
        return cmul((hk[0, :, cols], hk[1, :, cols]), f)

    def backward_kernel(f, cols):
        return cmul_conj((hk[0, :, cols], hk[1, :, cols]), f)

    def residue(f, cols):
        g = f[0] * f[0] + f[1] * f[1] - pat[:, cols]
        return g * f[0], g * f[1]

    def pair(ref, *at):
        return (ref[(*at, 0)], ref[(*at, 1)])

    def entering(layer):
        return pair(lit) if layer == 0 else pair(wave, layer - 1)

    def first_columns(layer):
        for side in (0, 1):
            src, dst = rim_rows(layer)[side]
            arrive("ty", side, src, dst, slot_of(0, layer, side))
        send_columns(0, layer)

    def next_columns(layer):
        update_middle(layer)
        send_columns(2, layer)

    top = slices - 1
    prepare_probe()
    fetch_core.wait()
    first_columns(0)
    prepare_frequencies()
    fetch_tab.wait()
    for step in range(STEPS):
        columns, strips = 2 * step, 2 * step + 1
        bring = first_columns if step == 0 else next_columns
        if step > 0:
            bring(0)
        bring(1)
        for layer in range(top):
            place_columns(columns, layer)
            moved = through(cmul(entering(layer), pair(tile, layer)), forward_kernel)
            wave[layer, 0] = moved[0]
            wave[layer, 1] = moved[1]
            if layer + 2 <= top:
                bring(layer + 2)
        place_columns(columns, top)
        up = through(cmul(entering(top), pair(tile, top)), residue)
        last = step == STEPS - 1
        for layer in range(top, -1, -1):
            send_gradient(strips, layer, cmul_conj(entering(layer), up))
            if layer < top:
                sum_columns(strips, layer + 1)
                if last:
                    send_last(layer + 1)
                else:
                    send_middle(layer + 1, 0)
            if layer > 0:
                up = through(cmul_conj(pair(tile, layer), up), backward_kernel)
        sum_columns(strips, 0)
        if last:
            send_last(0)
        else:
            send_middle(0, 0)
            for layer in range(slices):
                send_middle(layer, 1)
    for layer in range(top, -1, -1):
        update_last(layer)

    for axis, side, src, dst, slot in pending:
        @pl.when(near[axis][side][0])
        def _():
            copy_of(axis, side, src, dst, slot).wait_send()


def shards(object_field, probe, propagator_phase, patterns, scan_positions):
    slices, _, core, _ = object_field.shape
    n = probe.shape[1]
    m = (n - core) // 2
    f32 = jnp.float32
    tables = jnp.asarray(dft_tables(n))
    vmem = pl.BlockSpec(memory_space=pltpu.VMEM)
    hbm = pl.BlockSpec(memory_space=pltpu.HBM)
    slots = 8 * slices * 2
    return pl.pallas_call(
        kernel,
        out_shape=jax.ShapeDtypeStruct(object_field.shape, f32),
        in_specs=[pl.BlockSpec(memory_space=pltpu.SMEM)] + [hbm] * 5,
        out_specs=vmem,
        scratch_shapes=[
            pltpu.VMEM((slices, 2, n, n), f32),
            pltpu.VMEM((2, n, n), f32),
            pltpu.VMEM((2, n, n), f32),
            pltpu.VMEM((n, n), f32),
            pltpu.VMEM((slices - 1, 2, n, n), f32),
            pltpu.VMEM((slices, 2, n, core), f32),
            pltpu.VMEM((2 * STEPS, slices, 2, n + m, core), f32),
            pltpu.VMEM((2 * STEPS, slices, 2, 2, n // 2, core), f32),
            pltpu.VMEM((2 * STEPS, slices, 2, 2, n // 2, core), f32),
            pltpu.VMEM((slices, 2, 2, 2 * m, core), f32),
            pltpu.VMEM((slices, 2, 2, m, core), f32),
            pltpu.VMEM((2, n, n), f32),
            pltpu.VMEM(tables.shape, jnp.bfloat16),
            pltpu.SemaphoreType.DMA((slots,)),
            pltpu.SemaphoreType.DMA((slots,)),
            pltpu.SemaphoreType.DMA((5,)),
        ],
        compiler_params=pltpu.CompilerParams(
            collective_id=0, has_side_effects=True, vmem_limit_bytes=63 * 1024 * 1024
        ),
        name="steps",
    )(scan_positions, object_field, probe, propagator_phase, patterns, tables)


def solution(mesh):
    placed = (
        P(None, None, "ty", "tx"),
        P(),
        P(),
        P("ty", "tx", None, None, None),
        P("ty", "tx", None, None),
    )
    return jax.shard_map(
        shards, mesh=mesh, in_specs=placed, out_specs=P(None, None, "ty", "tx"), check_vma=False
    )
```

```python
import functools

import jax
import jax.numpy as jnp
import ml_dtypes
import numpy as np
from jax import lax
from jax.experimental import pallas as pl
from jax.experimental.pallas import tpu as pltpu
from jax.sharding import PartitionSpec as P

STEPS = 2

step_size = 0.05


def dft_tables(n):
    h = n // 2
    place = np.arange(h)
    tables = []
    for parity in (0, 1):
        turns = ((2 * place[:, None] + parity) * place[None, :]) % n
        angle = turns * (2.0 * np.pi / n)
        c = np.cos(angle) / np.sqrt(n)
        s = -np.sin(angle) / np.sqrt(n)
        block = np.block([[c, -s], [s, c]])
        for full in (block, block.T):
            high = full.astype(ml_dtypes.bfloat16)
            low = (full - high.astype(np.float64)).astype(ml_dtypes.bfloat16)
            tables += [high, low]
    return np.stack(tables)


def split2(x):
    high = x.astype(jnp.bfloat16)
    low = (x - high.astype(jnp.float32)).astype(jnp.bfloat16)
    return high, low


def split3(x):
    high = x.astype(jnp.bfloat16)
    rest = x - high.astype(jnp.float32)
    middle = rest.astype(jnp.bfloat16)
    low = (rest - middle.astype(jnp.float32)).astype(jnp.bfloat16)
    return high, middle, low


def dot(a, b):
    return jnp.dot(a, b, preferred_element_type=jnp.float32)


def cat(parts, axis):
    return jnp.concatenate(parts, axis=axis)


def cmul(a, b):
    return (a[0] * b[0] - a[1] * b[1], a[0] * b[1] + a[1] * b[0])


def cmul_conj(a, b):
    return (a[0] * b[0] + a[1] * b[1], a[0] * b[1] - a[1] * b[0])


def sin_cos(x):
    y = x * 0.5
    z = y * y
    s = jnp.float32(-2.50521083854417e-08)
    for c in (2.75573192239859e-06, -1.98412698412698e-04, 8.33333333333333e-03, -1.66666666666667e-01):
        s = s * z + jnp.float32(c)
    s = s * z * y + y
    c0 = jnp.float32(2.08767569878681e-09)
    for c in (-2.75573192239859e-07, 2.48015873015873e-05, -1.38888888888889e-03, 4.16666666666667e-02, -0.5):
        c0 = c0 * z + jnp.float32(c)
    c0 = c0 * z + 1.0
    return 2.0 * s * c0, 1.0 - 2.0 * s * s


def kernel(
    pos_ref, obj_ref, probe_hbm, phase_hbm, pat_hbm, tab_hbm, out_ref,
    tile, lit, hk, pat, wave, grad, rim, sendx, recvx, recvy, recvl,
    probe_ref, tab_ref, field, sem_s, sem_r, sem_in,
):
    slices = obj_ref.shape[0]
    core = obj_ref.shape[2]
    n = probe_ref.shape[1]
    h = n // 2
    m = (n - core) // 2
    ty, tx = lax.axis_index("ty"), lax.axis_index("tx")
    ny, nx = lax.axis_size("ty"), lax.axis_size("tx")
    near = {
        "ty": ((ty > 0, (ty - 1, tx)), (ty < ny - 1, (ty + 1, tx))),
        "tx": ((tx > 0, (ty, tx - 1)), (tx < nx - 1, (ty, tx + 1))),
    }
    pending = {}

    def copy_of(axis, side, src, dst, slot):
        return pltpu.make_async_remote_copy(
            src_ref=src, dst_ref=dst,
            send_sem=sem_s.at[slot], recv_sem=sem_r.at[slot],
            device_id=near[axis][side][1], device_id_type=pl.DeviceIdType.MESH,
        )

    def send(axis, side, ends, slot):
        @pl.when(near[axis][side][0])
        def _():
            copy_of(axis, side, *ends(), slot).start()

        pending[slot] = (axis, side, ends)

    def arrive(axis, side, src, dst, slot):
        @pl.when(near[axis][1 - side][0])
        def _():
            copy_of(axis, 1 - side, src, dst, slot).wait_recv()

    def slot_of(phase, layer, side):
        return (phase * slices + layer) * 2 + side

    fetch_core, fetch_probe, fetch_phase, fetch_pat, fetch_tab = (
        pltpu.make_async_copy(src, dst, sem_in.at[i])
        for i, (src, dst) in enumerate((
            (obj_ref, tile.at[:, :, pl.ds(0, core), pl.ds(0, core)]),
            (probe_hbm, probe_ref),
            (phase_hbm, hk.at[0]),
            (pat_hbm.at[0, 0, 0], pat),
            (tab_hbm, tab_ref),
        ))
    )
    for fetch in (fetch_core, fetch_probe, fetch_phase, fetch_pat, fetch_tab):
        fetch.start()

    barrier = pltpu.get_barrier_semaphore()
    count = jnp.int32(0)
    for axis in ("ty", "tx"):
        for there, device in near[axis]:
            @pl.when(there)
            def _():
                pl.semaphore_signal(barrier, inc=1, device_id=device, device_id_type=pl.DeviceIdType.MESH)
            count = count + there.astype(jnp.int32)
    pl.semaphore_wait(barrier, count)

    after, before = pl.ds(core, m), pl.ds(core + m, m)
    head, tail = pl.ds(0, m), pl.ds(core - m, m)
    own = pl.ds(0, core)
    other = pl.ds(core, core)

    def rim_rows(layer):
        return (
            (obj_ref.at[layer, :, head, :], tile.at[layer, :, after, own]),
            (obj_ref.at[layer, :, tail, :], tile.at[layer, :, before, own]),
        )

    def send_rim(layer):
        for side in (0, 1):
            send("ty", side, lambda side=side: rim_rows(layer)[side], slot_of(0, layer, side))

    send_rim(0)

    @pl.when(ty == 0)
    def _():
        tile[:, :, before, own] = jnp.zeros((slices, 2, m, core), jnp.float32)
        recvy[:, 1] = jnp.zeros(recvy.shape[:1] + recvy.shape[2:], jnp.float32)
        recvl[:, 1] = jnp.zeros(recvl.shape[:1] + recvl.shape[2:], jnp.float32)

    @pl.when(ty == ny - 1)
    def _():
        tile[:, :, after, own] = jnp.zeros((slices, 2, m, core), jnp.float32)
        recvy[:, 0] = jnp.zeros(recvy.shape[:1] + recvy.shape[2:], jnp.float32)
        recvl[:, 0] = jnp.zeros(recvl.shape[:1] + recvl.shape[2:], jnp.float32)

    @pl.when(tx == 0)
    def _():
        for phase in range(recvx.shape[0]):
            recvx[phase, :, 1] = jnp.zeros(recvx.shape[1:2] + recvx.shape[3:], jnp.float32)

    @pl.when(tx == nx - 1)
    def _():
        for phase in range(recvx.shape[0]):
            recvx[phase, :, 0] = jnp.zeros(recvx.shape[1:2] + recvx.shape[3:], jnp.float32)

    first_half = lax.broadcasted_iota(jnp.int32, (h, core), 1) < m

    def turn(x):
        return pltpu.roll(x, m, 1)

    def pack(block):
        top, bottom = block[:h], block[h:]
        return (
            jnp.where(first_half, top, turn(bottom)),
            jnp.where(first_half, turn(top), bottom),
        )

    def unpack(low, high):
        return (
            jnp.where(first_half, low, turn(high)),
            jnp.where(first_half, turn(low), high),
        )

    def send_strips(phase, layer, part, low, high, low_side):
        sendx[phase, layer, low_side, part] = low
        sendx[phase, layer, 1 - low_side, part] = high

    def start_strips(phase, layer):
        for side in (0, 1):
            send(
                "tx", side, lambda side=side: (sendx.at[phase, layer, side], recvx.at[phase, layer, side]),
                slot_of(2 * phase + 1, layer, side),
            )

    def wait_strips(phase, layer):
        for side in (0, 1):
            arrive("tx", side, sendx.at[phase, layer, side], recvx.at[phase, layer, side], slot_of(2 * phase + 1, layer, side))

    def send_columns(phase, layer):
        for part in (0, 1):
            low, high = pack(tile[layer, part, :, own])
            send_strips(phase, layer, part, low, high, 0)
        start_strips(phase, layer)

    def place_columns(phase, layer):
        wait_strips(phase, layer)
        for part in (0, 1):
            top, bottom = unpack(recvx[phase, layer, 0, part], recvx[phase, layer, 1, part])
            tile[layer, part, pl.ds(0, h), other] = top
            tile[layer, part, pl.ds(h, h), other] = bottom

    def send_gradient(phase, layer, g):
        for part in (0, 1):
            grad[layer, part, pl.ds(0, n)] = g[part][:, :core]
            low, high = pack(g[part][:, core:])
            send_strips(phase, layer, part, low, high, 1)
        start_strips(phase, layer)

    def sum_columns(phase, layer):
        wait_strips(phase, layer)
        for part in (0, 1):
            top, bottom = unpack(recvx[phase, layer, 1, part], recvx[phase, layer, 0, part])
            top = grad[layer, part, pl.ds(0, h)] + top
            rim[phase, layer, part, pl.ds(0, h)] = top
            rim[phase, layer, part, pl.ds(h, h)] = grad[layer, part, pl.ds(h, h)] + bottom
            rim[phase, layer, part, pl.ds(n, m)] = top[:m]

    def middle_rows(layer, part):
        return (
            (rim.at[1, layer, part, pl.ds(core + m, 2 * m), :], recvy.at[layer, 0, part]),
            (rim.at[1, layer, part, pl.ds(core - m, 2 * m), :], recvy.at[layer, 1, part]),
        )

    def last_rows(layer):
        return (
            (rim.at[3, layer, :, pl.ds(core + m, m), :], recvl.at[layer, 0]),
            (rim.at[3, layer, :, pl.ds(core, m), :], recvl.at[layer, 1]),
        )

    def send_middle(layer, part):
        for side in (0, 1):
            send("ty", side, lambda side=side: middle_rows(layer, part)[side], slot_of((2, 6)[part], layer, side))

    def send_last(layer):
        for side in (0, 1):
            send("ty", side, lambda side=side: last_rows(layer)[side], slot_of(4, layer, side))

    def update_middle(layer):
        for part in (0, 1):
            for side in (0, 1):
                src, dst = middle_rows(layer, part)[side]
                arrive("ty", side, src, dst, slot_of((2, 6)[part], layer, side))
            if part == 0 and layer + 1 < slices:
                send_middle(layer + 1, 1)
            for start, side, at in ((0, 1, m), (m, 0, 0), (2 * m, 0, m), (3 * m, 1, 0)):
                rows = pl.ds(start, m)
                total = rim[1, layer, part, rows] + recvy[layer, side, part, pl.ds(at, m)]
                tile[layer, part, rows, own] = tile[layer, part, rows, own] - step_size * total

        @pl.when(ty == 0)
        def _():
            tile[layer, :, before, own] = jnp.zeros((2, m, core), jnp.float32)

        @pl.when(ty == ny - 1)
        def _():
            tile[layer, :, after, own] = jnp.zeros((2, m, core), jnp.float32)

    def update_last(layer):
        for side in (0, 1):
            src, dst = last_rows(layer)[side]
            arrive("ty", side, src, dst, slot_of(4, layer, side))
        for part in (0, 1):
            for start, side in ((0, 1), (m, 0)):
                rows = pl.ds(start, m)
                total = rim[3, layer, part, rows] + recvl[layer, side, part]
                out_ref[layer, part, rows] = tile[layer, part, rows, own] - step_size * total

    row = lax.broadcasted_iota(jnp.int32, (n, n), 0)
    col = lax.broadcasted_iota(jnp.int32, (n, n), 1)

    def ones(mask):
        return jnp.where(mask, 1.0, 0.0).astype(jnp.bfloat16)

    def pick(left, x, right):
        a, b, c = split3(x)
        y = dot(left, a) + dot(left, b) + dot(left, c)
        a, b, c = split3(y)
        return dot(a, right) + dot(b, right) + dot(c, right)

    def rolled(i, j, shift):
        d = i - j + (m - shift + n)
        return ones((d == 0) | (d == n) | (d == 2 * n))

    def sorted_by_parity(i, j):
        return ones(jnp.where(i < h, 2 * i, 2 * i - n + 1) == j)

    def prepare_probe():
        fetch_probe.wait()
        roll_rows = rolled(row, col, pos_ref[0, 0, 0, 0])
        roll_cols = rolled(col, row, pos_ref[0, 0, 0, 1])
        for part in (0, 1):
            lit[part] = pick(roll_rows, probe_ref[part], roll_cols)

    def prepare_frequencies():
        by_row, by_col = sorted_by_parity(row, col), sorted_by_parity(col, row)
        fetch_phase.wait()
        sine, cosine = sin_cos(pick(by_row, hk[0], by_col))
        hk[0] = cosine
        hk[1] = sine
        fetch_pat.wait()
        pat[...] = pick(by_row, pat[...], by_col)

    EVEN, EVEN_T, ODD, ODD_T = 0, 2, 4, 6

    def from_left(table, x):
        high, low = tab_ref[table], tab_ref[table + 1]
        xh, xl = split2(x)
        return dot(cat([high, high, low], 1), cat([xh, xl, xh], 0))

    def from_right(x, table):
        high, low = tab_ref[table], tab_ref[table + 1]
        xh, xl = split2(x)
        return dot(cat([xh, xl, xh], 1), cat([high, high, low], 0))

    def through(stage):
        at_top = stage == slices - 1
        sign = jnp.where(at_top, 0.0, jnp.where(stage < slices - 1, 1.0, -1.0)).astype(jnp.float32)

        def weigh(f, cols):
            power = f[0] * f[0] + f[1] * f[1] - pat[:, cols]
            return cmul((jnp.where(at_top, power, hk[0, :, cols]), sign * hk[1, :, cols]), f)

        re, im = field[0], field[1]
        even = from_left(EVEN, cat([re[:h] + re[h:], im[:h] + im[h:]], 0))
        odd = from_left(ODD, cat([re[:h] - re[h:], im[:h] - im[h:]], 0))
        re = cat([even[:h], odd[:h]], 0)
        im = cat([even[h:], odd[h:]], 0)
        even = from_right(cat([re[:, :h] + re[:, h:], im[:, :h] + im[:, h:]], 1), EVEN_T)
        odd = from_right(cat([re[:, :h] - re[:, h:], im[:, :h] - im[:, h:]], 1), ODD_T)
        even = cat(weigh((even[:, :h], even[:, h:]), pl.ds(0, h)), 1)
        odd = cat(weigh((odd[:, :h], odd[:, h:]), pl.ds(h, h)), 1)
        even = from_right(even, EVEN)
        odd = from_right(odd, ODD)
        first, second = even + odd, even - odd
        re = cat([first[:, :h], second[:, :h]], 1)
        im = cat([first[:, h:], second[:, h:]], 1)
        even = from_left(EVEN_T, cat([re[:h], im[:h]], 0))
        odd = from_left(ODD_T, cat([re[h:], im[h:]], 0))
        first, second = even + odd, even - odd
        field[0] = cat([first[:h], second[:h]], 0)
        field[1] = cat([first[h:], second[h:]], 0)

    def pair(ref, *at):
        return (ref[(*at, 0)], ref[(*at, 1)])

    def entering(layer):
        return pair(lit) if layer == 0 else pair(wave, layer - 1)

    def first_columns(layer):
        for side in (0, 1):
            src, dst = rim_rows(layer)[side]
            arrive("ty", side, src, dst, slot_of(0, layer, side))
        send_columns(0, layer)

    def next_columns(layer):
        update_middle(layer)
        send_columns(2, layer)

    top = slices - 1
    stages = 2 * slices - 1

    def put(value):
        field[0] = value[0]
        field[1] = value[1]

    def ahead(step, stage):
        if stage <= top:
            if stage == 0 and step > 0:
                next_columns(0)
            if stage == 0:
                (next_columns if step else first_columns)(1)
            place_columns(2 * step, stage)
            put(cmul(entering(stage), pair(tile, stage)))
        else:
            put(cmul_conj(pair(tile, 2 * top - stage + 1), pair(field)))

    def behind(step, stage):
        last = step == STEPS - 1
        if stage < top:
            wave[stage] = field[...]
            if stage + 2 <= top:
                (next_columns if step else first_columns)(stage + 2)
            return
        layer = 2 * top - stage
        send_gradient(2 * step + 1, layer, cmul_conj(entering(layer), pair(field)))
        for done in ([layer + 1] if layer < top else []) + ([0] if layer == 0 else []):
            sum_columns(2 * step + 1, done)
            if last:
                send_last(done)
            else:
                send_middle(done, 0)
        if layer == 0 and not last:
            send_middle(0, 1)

    prepare_probe()
    fetch_core.wait()
    send_rim(1)
    first_columns(0)
    for layer in range(2, slices):
        send_rim(layer)
    prepare_frequencies()
    fetch_tab.wait()

    def turn_of(i, carry):
        for step in range(STEPS):
            for stage in range(stages):
                pl.when(i == step * stages + stage)(functools.partial(ahead, step, stage))
        through(lax.rem(i, stages))
        for step in range(STEPS):
            for stage in range(stages):
                pl.when(i == step * stages + stage)(functools.partial(behind, step, stage))
        return carry

    lax.fori_loop(0, STEPS * stages, turn_of, 0)
    for layer in range(top, -1, -1):
        update_last(layer)

    for slot, (axis, side, ends) in pending.items():
        @pl.when(near[axis][side][0])
        def _():
            copy_of(axis, side, *ends(), slot).wait_send()


def shards(object_field, probe, propagator_phase, patterns, scan_positions):
    slices, _, core, _ = object_field.shape
    n = probe.shape[1]
    m = (n - core) // 2
    f32 = jnp.float32
    tables = jnp.asarray(dft_tables(n))
    vmem = pl.BlockSpec(memory_space=pltpu.VMEM)
    hbm = pl.BlockSpec(memory_space=pltpu.HBM)
    slots = 8 * slices * 2
    return pl.pallas_call(
        kernel,
        out_shape=jax.ShapeDtypeStruct(object_field.shape, f32),
        in_specs=[pl.BlockSpec(memory_space=pltpu.SMEM)] + [hbm] * 5,
        out_specs=vmem,
        scratch_shapes=[
            pltpu.VMEM((slices, 2, n, n), f32),
            pltpu.VMEM((2, n, n), f32),
            pltpu.VMEM((2, n, n), f32),
            pltpu.VMEM((n, n), f32),
            pltpu.VMEM((slices - 1, 2, n, n), f32),
            pltpu.VMEM((slices, 2, n, core), f32),
            pltpu.VMEM((2 * STEPS, slices, 2, n + m, core), f32),
            pltpu.VMEM((2 * STEPS, slices, 2, 2, n // 2, core), f32),
            pltpu.VMEM((2 * STEPS, slices, 2, 2, n // 2, core), f32),
            pltpu.VMEM((slices, 2, 2, 2 * m, core), f32),
            pltpu.VMEM((slices, 2, 2, m, core), f32),
            pltpu.VMEM((2, n, n), f32),
            pltpu.VMEM(tables.shape, jnp.bfloat16),
            pltpu.VMEM((2, n, n), f32),
            pltpu.SemaphoreType.DMA((slots,)),
            pltpu.SemaphoreType.DMA((slots,)),
            pltpu.SemaphoreType.DMA((5,)),
        ],
        compiler_params=pltpu.CompilerParams(
            collective_id=0, has_side_effects=True, vmem_limit_bytes=63 * 1024 * 1024
        ),
        name="steps",
    )(scan_positions, object_field, probe, propagator_phase, patterns, tables)


def solution(mesh):
    placed = (
        P(None, None, "ty", "tx"),
        P(),
        P(),
        P("ty", "tx", None, None, None),
        P("ty", "tx", None, None),
    )
    return jax.shard_map(
        shards, mesh=mesh, in_specs=placed, out_specs=P(None, None, "ty", "tx"), check_vma=False
    )
```

```python
import functools

import jax
import jax.numpy as jnp
import ml_dtypes
import numpy as np
from jax import lax
from jax.experimental import pallas as pl
from jax.experimental.pallas import tpu as pltpu
from jax.sharding import PartitionSpec as P

STEPS = 2

step_size = 0.05


def dft_tables(n):
    h = n // 2
    place = np.arange(h)
    tables = []
    for parity in (0, 1):
        turns = ((2 * place[:, None] + parity) * place[None, :]) % n
        angle = turns * (2.0 * np.pi / n)
        c = np.cos(angle) / np.sqrt(n)
        s = -np.sin(angle) / np.sqrt(n)
        block = np.block([[c, -s], [s, c]])
        for full in (block, block.T):
            high = full.astype(ml_dtypes.bfloat16)
            low = (full - high.astype(np.float64)).astype(ml_dtypes.bfloat16)
            tables += [high, low]
    return np.stack(tables)


def split2(x):
    high = x.astype(jnp.bfloat16)
    low = (x - high.astype(jnp.float32)).astype(jnp.bfloat16)
    return high, low


def split3(x):
    high = x.astype(jnp.bfloat16)
    rest = x - high.astype(jnp.float32)
    middle = rest.astype(jnp.bfloat16)
    low = (rest - middle.astype(jnp.float32)).astype(jnp.bfloat16)
    return high, middle, low


def dot(a, b):
    return jnp.dot(a, b, preferred_element_type=jnp.float32)


def cat(parts, axis):
    return jnp.concatenate(parts, axis=axis)


def cmul(a, b):
    return (a[0] * b[0] - a[1] * b[1], a[0] * b[1] + a[1] * b[0])


def cmul_conj(a, b):
    return (a[0] * b[0] + a[1] * b[1], a[0] * b[1] - a[1] * b[0])


def sin_cos(x):
    y = x * 0.5
    z = y * y
    s = jnp.float32(-2.50521083854417e-08)
    for c in (2.75573192239859e-06, -1.98412698412698e-04, 8.33333333333333e-03, -1.66666666666667e-01):
        s = s * z + jnp.float32(c)
    s = s * z * y + y
    c0 = jnp.float32(2.08767569878681e-09)
    for c in (-2.75573192239859e-07, 2.48015873015873e-05, -1.38888888888889e-03, 4.16666666666667e-02, -0.5):
        c0 = c0 * z + jnp.float32(c)
    c0 = c0 * z + 1.0
    return 2.0 * s * c0, 1.0 - 2.0 * s * s


def kernel(
    pos_ref, obj_ref, probe_hbm, phase_hbm, pat_hbm, tab_hbm, out_ref,
    tile, lit, hk, pat, wave, grad, rim, sendx, recvx, recvy, recvl,
    probe_ref, tab_ref, field, sem_s, sem_r, sem_in,
):
    slices = obj_ref.shape[0]
    core = obj_ref.shape[2]
    n = probe_ref.shape[1]
    h = n // 2
    m = (n - core) // 2
    ty, tx = lax.axis_index("ty"), lax.axis_index("tx")
    ny, nx = lax.axis_size("ty"), lax.axis_size("tx")
    near = {
        "ty": ((ty > 0, (ty - 1, tx)), (ty < ny - 1, (ty + 1, tx))),
        "tx": ((tx > 0, (ty, tx - 1)), (tx < nx - 1, (ty, tx + 1))),
    }
    pending = {}

    def copy_of(axis, side, src, dst, slot):
        return pltpu.make_async_remote_copy(
            src_ref=src, dst_ref=dst,
            send_sem=sem_s.at[slot], recv_sem=sem_r.at[slot],
            device_id=near[axis][side][1], device_id_type=pl.DeviceIdType.MESH,
        )

    def send(axis, side, ends, slot):
        @pl.when(near[axis][side][0])
        def _():
            copy_of(axis, side, *ends(), slot).start()

        pending[slot] = (axis, side, ends)

    def arrive(axis, side, src, dst, slot):
        @pl.when(near[axis][1 - side][0])
        def _():
            copy_of(axis, 1 - side, src, dst, slot).wait_recv()

    def slot_of(phase, layer, side):
        return (phase * slices + layer) * 2 + side

    fetch_core, fetch_probe, fetch_phase, fetch_pat, fetch_tab = (
        pltpu.make_async_copy(src, dst, sem_in.at[i])
        for i, (src, dst) in enumerate((
            (obj_ref, tile.at[:, :, pl.ds(0, core), pl.ds(0, core)]),
            (probe_hbm, probe_ref),
            (phase_hbm, hk.at[0]),
            (pat_hbm.at[0, 0, 0], pat),
            (tab_hbm, tab_ref),
        ))
    )
    for fetch in (fetch_core, fetch_probe, fetch_phase, fetch_pat, fetch_tab):
        fetch.start()

    barrier = pltpu.get_barrier_semaphore()
    count = jnp.int32(0)
    for axis in ("ty", "tx"):
        for there, device in near[axis]:
            @pl.when(there)
            def _():
                pl.semaphore_signal(barrier, inc=1, device_id=device, device_id_type=pl.DeviceIdType.MESH)
            count = count + there.astype(jnp.int32)
    pl.semaphore_wait(barrier, count)

    after, before = pl.ds(core, m), pl.ds(core + m, m)
    head, tail = pl.ds(0, m), pl.ds(core - m, m)
    own = pl.ds(0, core)
    other = pl.ds(core, core)

    def rim_rows(layer):
        return (
            (obj_ref.at[layer, :, head, :], tile.at[layer, :, after, own]),
            (obj_ref.at[layer, :, tail, :], tile.at[layer, :, before, own]),
        )

    def send_rim(layer):
        for side in (0, 1):
            send("ty", side, lambda side=side: rim_rows(layer)[side], slot_of(0, layer, side))

    send_rim(0)

    @pl.when(ty == 0)
    def _():
        tile[:, :, before, own] = jnp.zeros((slices, 2, m, core), jnp.float32)
        recvy[:, 1] = jnp.zeros(recvy.shape[:1] + recvy.shape[2:], jnp.float32)
        recvl[:, 1] = jnp.zeros(recvl.shape[:1] + recvl.shape[2:], jnp.float32)

    @pl.when(ty == ny - 1)
    def _():
        tile[:, :, after, own] = jnp.zeros((slices, 2, m, core), jnp.float32)
        recvy[:, 0] = jnp.zeros(recvy.shape[:1] + recvy.shape[2:], jnp.float32)
        recvl[:, 0] = jnp.zeros(recvl.shape[:1] + recvl.shape[2:], jnp.float32)

    @pl.when(tx == 0)
    def _():
        for phase in range(recvx.shape[0]):
            recvx[phase, :, 1] = jnp.zeros(recvx.shape[1:2] + recvx.shape[3:], jnp.float32)

    @pl.when(tx == nx - 1)
    def _():
        for phase in range(recvx.shape[0]):
            recvx[phase, :, 0] = jnp.zeros(recvx.shape[1:2] + recvx.shape[3:], jnp.float32)

    first_half = lax.broadcasted_iota(jnp.int32, (h, core), 1) < m

    def turn(x):
        return pltpu.roll(x, m, 1)

    def pack(block):
        top, bottom = block[:h], block[h:]
        return (
            jnp.where(first_half, top, turn(bottom)),
            jnp.where(first_half, turn(top), bottom),
        )

    def unpack(low, high):
        return (
            jnp.where(first_half, low, turn(high)),
            jnp.where(first_half, turn(low), high),
        )

    def send_strips(phase, layer, part, low, high, low_side):
        sendx[phase, layer, low_side, part] = low
        sendx[phase, layer, 1 - low_side, part] = high

    def start_strips(phase, layer):
        for side in (0, 1):
            send(
                "tx", side, lambda side=side: (sendx.at[phase, layer, side], recvx.at[phase, layer, side]),
                slot_of(2 * phase + 1, layer, side),
            )

    def wait_strips(phase, layer):
        for side in (0, 1):
            arrive("tx", side, sendx.at[phase, layer, side], recvx.at[phase, layer, side], slot_of(2 * phase + 1, layer, side))

    def send_columns(phase, layer):
        for part in (0, 1):
            low, high = pack(tile[layer, part, :, own])
            send_strips(phase, layer, part, low, high, 0)
        start_strips(phase, layer)

    def place_columns(phase, layer):
        wait_strips(phase, layer)
        for part in (0, 1):
            top, bottom = unpack(recvx[phase, layer, 0, part], recvx[phase, layer, 1, part])
            tile[layer, part, pl.ds(0, h), other] = top
            tile[layer, part, pl.ds(h, h), other] = bottom

    def send_gradient(phase, layer, g):
        for part in (0, 1):
            grad[layer, part, pl.ds(0, n)] = g[part][:, :core]
            low, high = pack(g[part][:, core:])
            send_strips(phase, layer, part, low, high, 1)
        start_strips(phase, layer)

    def sum_columns(phase, layer):
        wait_strips(phase, layer)
        for part in (0, 1):
            top, bottom = unpack(recvx[phase, layer, 1, part], recvx[phase, layer, 0, part])
            top = grad[layer, part, pl.ds(0, h)] + top
            rim[phase, layer, part, pl.ds(0, h)] = top
            rim[phase, layer, part, pl.ds(h, h)] = grad[layer, part, pl.ds(h, h)] + bottom
            rim[phase, layer, part, pl.ds(n, m)] = top[:m]

    def middle_rows(layer, part):
        return (
            (rim.at[1, layer, part, pl.ds(core + m, 2 * m), :], recvy.at[layer, 0, part]),
            (rim.at[1, layer, part, pl.ds(core - m, 2 * m), :], recvy.at[layer, 1, part]),
        )

    def last_rows(layer):
        return (
            (rim.at[3, layer, :, pl.ds(core + m, m), :], recvl.at[layer, 0]),
            (rim.at[3, layer, :, pl.ds(core, m), :], recvl.at[layer, 1]),
        )

    def send_middle(layer, part):
        for side in (0, 1):
            send("ty", side, lambda side=side: middle_rows(layer, part)[side], slot_of((2, 6)[part], layer, side))

    def send_last(layer):
        for side in (0, 1):
            send("ty", side, lambda side=side: last_rows(layer)[side], slot_of(4, layer, side))

    def update_middle(layer):
        for part in (0, 1):
            for side in (0, 1):
                src, dst = middle_rows(layer, part)[side]
                arrive("ty", side, src, dst, slot_of((2, 6)[part], layer, side))
            if part == 0 and layer + 1 < slices:
                send_middle(layer + 1, 1)
            for start, side, at in ((0, 1, m), (m, 0, 0), (2 * m, 0, m), (3 * m, 1, 0)):
                rows = pl.ds(start, m)
                total = rim[1, layer, part, rows] + recvy[layer, side, part, pl.ds(at, m)]
                tile[layer, part, rows, own] = tile[layer, part, rows, own] - step_size * total

        @pl.when(ty == 0)
        def _():
            tile[layer, :, before, own] = jnp.zeros((2, m, core), jnp.float32)

        @pl.when(ty == ny - 1)
        def _():
            tile[layer, :, after, own] = jnp.zeros((2, m, core), jnp.float32)

    def update_last(layer):
        for side in (0, 1):
            src, dst = last_rows(layer)[side]
            arrive("ty", side, src, dst, slot_of(4, layer, side))
        for part in (0, 1):
            for start, side in ((0, 1), (m, 0)):
                rows = pl.ds(start, m)
                total = rim[3, layer, part, rows] + recvl[layer, side, part]
                out_ref[layer, part, rows] = tile[layer, part, rows, own] - step_size * total

    row = lax.broadcasted_iota(jnp.int32, (n, n), 0)
    col = lax.broadcasted_iota(jnp.int32, (n, n), 1)

    def ones(mask):
        return jnp.where(mask, 1.0, 0.0).astype(jnp.bfloat16)

    def pick(left, x, right):
        a, b, c = split3(x)
        y = dot(left, a) + dot(left, b) + dot(left, c)
        a, b, c = split3(y)
        return dot(a, right) + dot(b, right) + dot(c, right)

    def rolled(i, j, shift):
        d = i - j + (m - shift + n)
        return ones((d == 0) | (d == n) | (d == 2 * n))

    def sorted_by_parity(i, j):
        return ones(jnp.where(i < h, 2 * i, 2 * i - n + 1) == j)

    def prepare_probe():
        fetch_probe.wait()
        roll_rows = rolled(row, col, pos_ref[0, 0, 0, 0])
        roll_cols = rolled(col, row, pos_ref[0, 0, 0, 1])
        for part in (0, 1):
            lit[part] = pick(roll_rows, probe_ref[part], roll_cols)

    def prepare_frequencies():
        by_row, by_col = sorted_by_parity(row, col), sorted_by_parity(col, row)
        fetch_phase.wait()
        sine, cosine = sin_cos(pick(by_row, hk[0], by_col))
        hk[0] = cosine
        hk[1] = sine
        fetch_pat.wait()
        pat[...] = pick(by_row, pat[...], by_col)

    EVEN, EVEN_T, ODD, ODD_T = 0, 2, 4, 6

    def from_left(table, x):
        high, low = tab_ref[table], tab_ref[table + 1]
        xh, xl = split2(x)
        both = dot(cat([high, low], 0), xh)
        return both[:n] + (both[n:] + dot(high, xl))

    def from_right(x, table):
        high, low = tab_ref[table], tab_ref[table + 1]
        xh, xl = split2(x)
        both = dot(cat([xh, xl], 0), high)
        return both[:n] + (both[n:] + dot(xh, low))

    def through(stage):
        at_top = stage == slices - 1
        sign = jnp.where(at_top, 0.0, jnp.where(stage < slices - 1, 1.0, -1.0)).astype(jnp.float32)

        def weigh(f, cols):
            power = f[0] * f[0] + f[1] * f[1] - pat[:, cols]
            return cmul((jnp.where(at_top, power, hk[0, :, cols]), sign * hk[1, :, cols]), f)

        re, im = field[0], field[1]
        even = from_left(EVEN, cat([re[:h] + re[h:], im[:h] + im[h:]], 0))
        odd = from_left(ODD, cat([re[:h] - re[h:], im[:h] - im[h:]], 0))
        re = cat([even[:h], odd[:h]], 0)
        im = cat([even[h:], odd[h:]], 0)
        even = from_right(cat([re[:, :h] + re[:, h:], im[:, :h] + im[:, h:]], 1), EVEN_T)
        odd = from_right(cat([re[:, :h] - re[:, h:], im[:, :h] - im[:, h:]], 1), ODD_T)
        even = cat(weigh((even[:, :h], even[:, h:]), pl.ds(0, h)), 1)
        odd = cat(weigh((odd[:, :h], odd[:, h:]), pl.ds(h, h)), 1)
        even = from_right(even, EVEN)
        odd = from_right(odd, ODD)
        first, second = even + odd, even - odd
        re = cat([first[:, :h], second[:, :h]], 1)
        im = cat([first[:, h:], second[:, h:]], 1)
        even = from_left(EVEN_T, cat([re[:h], im[:h]], 0))
        odd = from_left(ODD_T, cat([re[h:], im[h:]], 0))
        first, second = even + odd, even - odd
        field[0] = cat([first[:h], second[:h]], 0)
        field[1] = cat([first[h:], second[h:]], 0)

    def pair(ref, *at):
        return (ref[(*at, 0)], ref[(*at, 1)])

    def entering(layer):
        return pair(lit) if layer == 0 else pair(wave, layer - 1)

    def first_columns(layer):
        for side in (0, 1):
            src, dst = rim_rows(layer)[side]
            arrive("ty", side, src, dst, slot_of(0, layer, side))
        send_columns(0, layer)

    def next_columns(layer):
        update_middle(layer)
        send_columns(2, layer)

    top = slices - 1
    stages = 2 * slices - 1

    def put(value):
        field[0] = value[0]
        field[1] = value[1]

    def ahead(step, stage):
        if stage <= top:
            if stage == 0 and step > 0:
                next_columns(0)
            if stage == 0:
                (next_columns if step else first_columns)(1)
            place_columns(2 * step, stage)
            put(cmul(entering(stage), pair(tile, stage)))
        else:
            put(cmul_conj(pair(tile, 2 * top - stage + 1), pair(field)))

    def behind(step, stage):
        last = step == STEPS - 1
        if stage < top:
            wave[stage] = field[...]
            if stage + 2 <= top:
                (next_columns if step else first_columns)(stage + 2)
            return
        layer = 2 * top - stage
        send_gradient(2 * step + 1, layer, cmul_conj(entering(layer), pair(field)))
        for done in ([layer + 1] if layer < top else []) + ([0] if layer == 0 else []):
            sum_columns(2 * step + 1, done)
            if last:
                send_last(done)
            else:
                send_middle(done, 0)
        if layer == 0 and not last:
            send_middle(0, 1)

    prepare_probe()
    fetch_core.wait()
    send_rim(1)
    first_columns(0)
    for layer in range(2, slices):
        send_rim(layer)
    prepare_frequencies()
    fetch_tab.wait()

    def turn_of(i, carry):
        for step in range(STEPS):
            for stage in range(stages):
                pl.when(i == step * stages + stage)(functools.partial(ahead, step, stage))
        through(lax.rem(i, stages))
        for step in range(STEPS):
            for stage in range(stages):
                pl.when(i == step * stages + stage)(functools.partial(behind, step, stage))
        return carry

    lax.fori_loop(0, STEPS * stages, turn_of, 0)
    for layer in range(top, -1, -1):
        update_last(layer)

    for slot, (axis, side, ends) in pending.items():
        @pl.when(near[axis][side][0])
        def _():
            copy_of(axis, side, *ends(), slot).wait_send()


def shards(object_field, probe, propagator_phase, patterns, scan_positions):
    slices, _, core, _ = object_field.shape
    n = probe.shape[1]
    m = (n - core) // 2
    f32 = jnp.float32
    tables = jnp.asarray(dft_tables(n))
    vmem = pl.BlockSpec(memory_space=pltpu.VMEM)
    hbm = pl.BlockSpec(memory_space=pltpu.HBM)
    slots = 8 * slices * 2
    return pl.pallas_call(
        kernel,
        out_shape=jax.ShapeDtypeStruct(object_field.shape, f32),
        in_specs=[pl.BlockSpec(memory_space=pltpu.SMEM)] + [hbm] * 5,
        out_specs=vmem,
        scratch_shapes=[
            pltpu.VMEM((slices, 2, n, n), f32),
            pltpu.VMEM((2, n, n), f32),
            pltpu.VMEM((2, n, n), f32),
            pltpu.VMEM((n, n), f32),
            pltpu.VMEM((slices - 1, 2, n, n), f32),
            pltpu.VMEM((slices, 2, n, core), f32),
            pltpu.VMEM((2 * STEPS, slices, 2, n + m, core), f32),
            pltpu.VMEM((2 * STEPS, slices, 2, 2, n // 2, core), f32),
            pltpu.VMEM((2 * STEPS, slices, 2, 2, n // 2, core), f32),
            pltpu.VMEM((slices, 2, 2, 2 * m, core), f32),
            pltpu.VMEM((slices, 2, 2, m, core), f32),
            pltpu.VMEM((2, n, n), f32),
            pltpu.VMEM(tables.shape, jnp.bfloat16),
            pltpu.VMEM((2, n, n), f32),
            pltpu.SemaphoreType.DMA((slots,)),
            pltpu.SemaphoreType.DMA((slots,)),
            pltpu.SemaphoreType.DMA((5,)),
        ],
        compiler_params=pltpu.CompilerParams(
            collective_id=0, has_side_effects=True, vmem_limit_bytes=63 * 1024 * 1024
        ),
        name="steps",
    )(scan_positions, object_field, probe, propagator_phase, patterns, tables)


def solution(mesh):
    placed = (
        P(None, None, "ty", "tx"),
        P(),
        P(),
        P("ty", "tx", None, None, None),
        P("ty", "tx", None, None),
    )
    return jax.shard_map(
        shards, mesh=mesh, in_specs=placed, out_specs=P(None, None, "ty", "tx"), check_vma=False
    )
```
